256 devices in a mesh: seq: 32 (over x, z_lo, core), ex: 8 (over y, z_hi).
Axes of the slice: x: 4, y: 4, z: 8 (z_hi: 2, z_lo: 4; z = z_hi * 4 + z_lo), core: 2. Of those that a mesh axis runs over, the one named last changes fastest.
Arguments:
- acts: bfloat16 [16, 2048, 4096], P('ex', 'seq'), may hold values from -6 to 6
- out_grads: bfloat16 [16, 2048, 5120], P('ex', 'seq'), may hold values from -6 to 6
- lengths: int32 [16], P('ex'), may hold values from 512 to 2048, as said below
- in_tiles: bfloat16 [32, 128, 128], replicated, may hold values from -0.09375 to 0.09375
- in_blocks: int32 [32], replicated, may hold values from 0 to 31, each once
- in_signs: int32 [32, 128], replicated, may hold values 0 or 1
- out_tiles: bfloat16 [40, 128, 64], replicated, may hold values from -0.09375 to 0.09375
- out_blocks: int32 [40], replicated, may hold values from 0 to 39, as said below
- out_signs: int32 [40, 128], replicated, may hold values 0 or 1
- query_grads: bfloat16 [4096, 8192], P('seq', 'ex'), may hold values from -6 to 6
Outputs:
- scores: float32 [16, 4096], P('ex', 'seq')
The draws below stay inside these ranges and needn't reach their ends.
Inputs may be any that keep to these rules, and one draw needn't show every extreme that they name: `lengths`: every training sequence has at least 512 live positions and some sequence has all 2048. `in_blocks`: a permutation of the 32 input feature blocks. `out_blocks`: the first 32 entries are a permutation of 0 to 31, the last 8 a permutation of 32 to 39.
All inputs are finite; a program needn't handle non-finite values.
Results may differ from the reference program's by a relative error of at most 0.005.
Values may be sent and summed in bfloat16 or wider, within the bound.
No kernel may reach another device: no remote copies, remote signals or barrier semaphores. Data moves between devices by JAX's collectives and lax.ppermute only.
A program may use at most 64 MiB of HBM per device.

```python
import jax
import jax.numpy as jnp
from jax import lax

D = 4096
KV = 1024
S = 2048
KI = 64
KO = 64
EXAMPLES = 16
QUERIES = 4096
PROJ = 8192


def draw_lengths(key, part):
    base = jax.random.randint(jax.random.fold_in(key, 11), (EXAMPLES,), S // 4, S + 1)
    longest = jax.random.randint(jax.random.fold_in(key, 12), (), 0, EXAMPLES)
    return jnp.where(jnp.arange(EXAMPLES) == longest, S, base).astype(jnp.int32)


def draw_out_blocks(key, part):
    upper = jax.random.permutation(jax.random.fold_in(key, 21), D // 128)
    lower = D // 128 + jax.random.permutation(jax.random.fold_in(key, 22), KV // 128)
    return jnp.concatenate([upper, lower]).astype(jnp.int32)


def plant(array, stream_key, smallest, largest):
    longest = array.shape.index(max(array.shape))
    spots = []
    for shift in (0, 1):
        where = [jax.random.randint(jax.random.fold_in(stream_key, axis), (), 0, length) for axis, length in enumerate(array.shape)]
        where[longest] = (where[longest] + shift) % array.shape[longest]
        spots.append(tuple(where))
    return array.at[spots[0]].set(smallest).at[spots[1]].set(largest)


def block_levels(own_key, extent, cuts, smallest, largest):
    def one(axis_at, parts):
        heights = jax.random.uniform(jax.random.fold_in(jax.random.fold_in(own_key, 6), axis_at), (parts,), jnp.float32, smallest / len(cuts), largest / len(cuts))
        return jnp.repeat(jnp.exp(heights), extent[axis_at] // parts).reshape((-1,) + (1,) * (len(extent) - axis_at - 1))

    factor_of = one(*cuts[0])
    for cut in cuts[1:]:
        factor_of = factor_of * one(*cut)
    return factor_of


def gaussian(stream_key, dims, spread, most, pieces=(), kind=jnp.bfloat16):
    drawn = jax.random.normal(stream_key, dims, jnp.float32) * spread
    if len(pieces) > 0:
        drawn = block_levels(stream_key, dims, pieces, -0.22, 0.18) * drawn
    return jnp.clip(drawn, min=-most, max=most).astype(kind)


def setup_inputs(seed: int = 0) -> dict:
    key_list = jax.random.split(jax.random.key(seed), 11)
    return {
        "acts": gaussian(key_list[0], (EXAMPLES, S, D), 1.0, 6.0, ((0, 8), (1, 32))),
        "out_grads": gaussian(key_list[1], (EXAMPLES, S, D + KV), 1.0, 6.0, ((0, 8), (1, 32))),
        "lengths": draw_lengths(jax.random.fold_in(key_list[10], 71), 0),
        "in_tiles": gaussian(key_list[3], (D // 128, 128, 2 * KI), D ** -0.5, 0.09375),
        "in_blocks": jax.random.permutation(key_list[4], D // 128).astype(jnp.int32),
        "in_signs": plant((jax.random.randint(key_list[5], (D // 128, 128), 0, 2) < 1).astype(jnp.int32), jax.random.fold_in(key_list[5], 1), 0, 1),
        "out_tiles": gaussian(key_list[6], ((D + KV) // 128, 128, KO), D ** -0.5, 0.09375),
        "out_blocks": draw_out_blocks(jax.random.fold_in(key_list[10], 71), 0),
        "out_signs": plant((jax.random.randint(key_list[8], ((D + KV) // 128, 128), 0, 2) < 1).astype(jnp.int32), jax.random.fold_in(key_list[8], 1), 0, 1),
        "query_grads": gaussian(key_list[9], (QUERIES, PROJ), 1.0, 6.0, ((0, 32), (1, 8))),
    }


def place(sketch_tiles, block_ids, sign_bits):
    signed = sketch_tiles.astype(jnp.float32) * (2 * sign_bits - 1).astype(jnp.float32)[:, :, None]
    placed = jnp.zeros_like(signed).at[block_ids].set(signed)
    return placed.reshape(-1, sketch_tiles.shape[2]).astype(jnp.bfloat16)


def widen(placed, split_at):
    out_cols = placed.shape[1]
    upper = jnp.concatenate([placed[:split_at], jnp.zeros((split_at, out_cols), jnp.bfloat16)], 1)
    lower = jnp.concatenate([jnp.zeros((placed.shape[0] - split_at, out_cols), jnp.bfloat16), placed[split_at:]], 1)
    return jnp.concatenate([upper, lower], 0)


def reference(acts, out_grads, lengths, in_tiles, in_blocks, in_signs, out_tiles, out_blocks, out_signs, query_grads):
    r_in = place(in_tiles, in_blocks, in_signs)
    r_out = widen(place(out_tiles, out_blocks, out_signs), D)
    positions = jnp.arange(S, dtype=jnp.int32)

    def per_example(example):
        act_rows, grad_rows, seq_length = example
        live_rows = (positions < seq_length).astype(jnp.float32)
        in_sketched = (jnp.dot(act_rows, r_in, preferred_element_type=jnp.float32) * live_rows[:, None]).astype(jnp.bfloat16)
        out_sketched = jnp.dot(grad_rows, r_out, preferred_element_type=jnp.float32).astype(jnp.bfloat16)
        crossed = jnp.dot(in_sketched.T, out_sketched, preferred_element_type=jnp.float32)
        joined = jnp.stack([crossed[:KI, :KO], crossed[KI:, KO:]], 0).reshape(-1)
        return joined / seq_length.astype(jnp.float32)

    train_proj = lax.map(per_example, (acts, out_grads, lengths)).astype(jnp.bfloat16)
    return jnp.dot(train_proj, query_grads.T, preferred_element_type=jnp.float32)
```

```python
import functools

import jax
import jax.numpy as jnp
from jax import lax
from jax.experimental import pallas as pl
from jax.experimental.pallas import tpu as pltpu
from jax.sharding import PartitionSpec as P

VMEM_LIMIT = 56 * 1024 * 1024
NT = (((1,), (1,)), ((), ()))


def sketch_kernel(
    acts_hbm,
    grads_hbm,
    lengths_hbm,
    in_tiles_hbm,
    in_blocks_hbm,
    in_signs_hbm,
    out_tiles_hbm,
    out_blocks_hbm,
    out_signs_hbm,
    partial_ref,
    acts,
    grads,
    lengths,
    in_tiles,
    in_blocks,
    in_signs,
    out_tiles,
    out_blocks,
    out_signs,
    sems,
):
    pairs = (
        (in_blocks_hbm, in_blocks),
        (in_signs_hbm, in_signs),
        (acts_hbm, acts),
        (in_tiles_hbm, in_tiles),
        (lengths_hbm, lengths),
        (out_blocks_hbm, out_blocks),
        (out_signs_hbm, out_signs),
        (grads_hbm, grads),
        (out_tiles_hbm, out_tiles),
    )
    copies = [pltpu.make_async_copy(src, dst, sems.at[i]) for i, (src, dst) in enumerate(pairs)]
    for copy in copies:
        copy.start()
    rows = acts.shape[0]
    examples = lengths.shape[0]
    seq_dev = rows // examples
    offset = lax.axis_index("seq") * seq_dev

    def gathered(source, blocks, signs, first, count):
        parts = []
        for b in range(first, first + count):
            start = pl.multiple_of(blocks[b] * 128, 128)
            sign = (2 * signs[b : b + 1, :] - 1).astype(jnp.float32).astype(jnp.bfloat16)
            parts.append(source[:, pl.ds(start, 128)] * sign)
        return jnp.concatenate(parts, axis=1)

    for copy in copies[:4]:
        copy.wait()
    in_sum = jnp.zeros((rows, 128), jnp.float32)
    step = 4
    for b in range(0, in_tiles.shape[0], step):
        in_sum += jnp.dot(
            gathered(acts, in_blocks, in_signs, b, step),
            in_tiles[b : b + step].reshape(step * 128, 128),
            preferred_element_type=jnp.float32,
        )
    copies[4].wait()
    row = lax.broadcasted_iota(jnp.int32, (rows, 128), 0)
    limit = jnp.full((rows, 128), lengths[0], jnp.int32)
    for e in range(1, examples):
        limit = jnp.where(row >= e * seq_dev, lengths[e], limit)
    live = (row % seq_dev + offset) < limit
    in_sketched = jnp.where(live, in_sum, 0.0).astype(jnp.bfloat16)
    src = lax.broadcasted_iota(jnp.int32, (128, 128), 1)
    dst = lax.broadcasted_iota(jnp.int32, (128, 128), 0)
    pick = (src == (dst // 64) * 64 + 2 * (dst % 32) + (dst // 32) % 2).astype(jnp.bfloat16)
    in_turned = lax.dot_general(pick, in_sketched, NT, preferred_element_type=jnp.float32)
    in_turned = in_turned.astype(jnp.bfloat16)

    for copy in copies[5:]:
        copy.wait()
    out_twice = []
    for first, last in ((0, in_tiles.shape[0]), (in_tiles.shape[0], out_tiles.shape[0])):
        out_sum = jnp.zeros((rows, 128), jnp.float32)
        for b in range(first, last, step):
            tile = jnp.concatenate([out_tiles[b + i] for i in range(step)], axis=1)
            out_sum += lax.dot_general(
                gathered(grads, out_blocks, out_signs, b, step),
                jnp.concatenate([tile, tile], axis=0),
                NT,
                preferred_element_type=jnp.float32,
            )
        out_twice.append(out_sum.astype(jnp.bfloat16))
    lane = lax.broadcasted_iota(jnp.int32, (32, 128), 1)
    for e in range(examples):
        at = slice(e * seq_dev, (e + 1) * seq_dev)
        for layer in range(2):
            both = jnp.dot(
                in_turned[layer * 64 : (layer + 1) * 64, at],
                out_twice[layer][at, :],
                preferred_element_type=jnp.float32,
            )
            flat = jnp.where(lane < 64, both[:32], both[32:])
            for j in range(4):
                partial_ref[layer * 4 + j, e * 8 : (e + 1) * 8, :] = flat[8 * j : 8 * j + 8]


def score_kernel(mine_ref, other_ref, *refs):
    queries, out_ref = refs[:-1], refs[-1]
    y = lax.axis_index("ex") // 2
    total = None
    for m, query in enumerate(queries):
        at = lax.bitwise_xor(y, m)
        rows = jnp.concatenate([mine_ref[at], other_ref[at]], axis=0).astype(jnp.float32)
        row = lax.broadcasted_iota(jnp.int32, rows.shape, 0)
        spread = jnp.concatenate(
            [jnp.where(row % 8 == r, rows, 0.0) for r in range(8)], axis=1
        ).astype(jnp.bfloat16)
        part = lax.dot_general(spread, query[...], NT, preferred_element_type=jnp.float32)
        total = part if total is None else total + part
    out_ref[...] = total.reshape(total.shape[0] // 8, 8, total.shape[1]).sum(1)


def swap(x, axis, mask):
    size = lax.axis_size(axis)
    return lax.ppermute(x, axis, [(i, i ^ mask) for i in range(size)])


def per_device(
    acts,
    out_grads,
    lengths,
    in_tiles,
    in_blocks,
    in_signs,
    out_tiles,
    out_blocks,
    out_signs,
    query_grads,
):
    examples_dev, seq_dev, width = acts.shape
    rows = examples_dev * seq_dev
    queries = [query_grads] + [swap(query_grads, "ex", m) for m in (2, 4, 6)]
    operands = (
        acts.reshape(rows, width),
        out_grads.reshape(rows, -1),
        lengths,
        in_tiles,
        in_blocks,
        in_signs,
        jnp.swapaxes(out_tiles, 1, 2),
        out_blocks,
        out_signs,
    )
    in_smem = (2, 4, 7)
    total = pl.pallas_call(
        sketch_kernel,
        out_shape=jax.ShapeDtypeStruct((8, examples_dev * 8, 128), jnp.float32),
        in_specs=[pl.BlockSpec(memory_space=pl.ANY)] * len(operands),
        out_specs=pl.BlockSpec(memory_space=pltpu.VMEM),
        scratch_shapes=[
            (pltpu.SMEM if i in in_smem else pltpu.VMEM)(x.shape, x.dtype)
            for i, x in enumerate(operands)
        ]
        + [pltpu.SemaphoreType.DMA((len(operands),))],
        compiler_params=pltpu.CompilerParams(vmem_limit_bytes=VMEM_LIMIT),
        name="sketch",
    )(*operands)
    for mask in (1, 2, 4, 8, 24):
        total = total + swap(total, "seq", mask)
    half = lax.axis_index("ex") % 2
    train = total.reshape(8, examples_dev, 8, 128) / lengths.astype(jnp.float32)[None, :, None, None]
    train = train.astype(jnp.bfloat16).reshape(4, 2, examples_dev * 8, 128)
    kept = lax.dynamic_index_in_dim(train, half, 1, keepdims=False)
    sent = lax.dynamic_index_in_dim(train, 1 - half, 1, keepdims=False)
    other = swap(sent, "ex", 1)
    scores = pl.pallas_call(
        score_kernel,
        out_shape=jax.ShapeDtypeStruct((2 * examples_dev, query_grads.shape[0]), jnp.float32),
        in_specs=[pl.BlockSpec(memory_space=pltpu.VMEM)] * 6,
        out_specs=pl.BlockSpec(memory_space=pltpu.VMEM),
        compiler_params=pltpu.CompilerParams(vmem_limit_bytes=VMEM_LIMIT),
        name="score",
    )(kept, other, *queries)
    return scores[:examples_dev] + swap(scores[examples_dev:], "ex", 1)


def solution(mesh):
    in_specs = (
        P("ex", "seq", None),
        P("ex", "seq", None),
        P("ex"),
        P(),
        P(),
        P(),
        P(),
        P(),
        P(),
        P("seq", "ex"),
    )
    out_specs = P("ex", "seq")
    return jax.shard_map(
        per_device, mesh=mesh, in_specs=in_specs, out_specs=out_specs, check_vma=False
    )
```

```python
import functools

import jax
import jax.numpy as jnp
from jax import lax
from jax.experimental import pallas as pl
from jax.experimental.pallas import tpu as pltpu
from jax.sharding import PartitionSpec as P

VMEM_LIMIT = 16 * 1024 * 1024
SCORE_VMEM = 8 * 1024 * 1024
NT = (((1,), (1,)), ((), ()))


def sketch_kernel(
    acts_hbm,
    grads_hbm,
    lengths_hbm,
    in_tiles_hbm,
    in_blocks_hbm,
    in_signs_hbm,
    out_tiles_hbm,
    out_blocks_hbm,
    out_signs_hbm,
    partial_ref,
    acts,
    grads,
    lengths,
    in_tiles,
    in_blocks,
    in_signs,
    out_tiles,
    out_blocks,
    out_signs,
    sems,
):
    pairs = (
        (in_blocks_hbm, in_blocks),
        (in_signs_hbm, in_signs),
        (acts_hbm, acts),
        (in_tiles_hbm, in_tiles),
        (lengths_hbm, lengths),
        (out_blocks_hbm, out_blocks),
        (out_signs_hbm, out_signs),
        (grads_hbm, grads),
        (out_tiles_hbm, out_tiles),
    )
    copies = [pltpu.make_async_copy(src, dst, sems.at[i]) for i, (src, dst) in enumerate(pairs)]
    for copy in copies:
        copy.start()
    rows = acts.shape[0]
    examples = lengths.shape[0]
    seq_dev = rows // examples
    offset = lax.axis_index("seq") * seq_dev

    def gathered(source, blocks, signs, first, count):
        parts = []
        for b in range(first, first + count):
            start = pl.multiple_of(blocks[b] * 128, 128)
            sign = (2 * signs[b : b + 1, :] - 1).astype(jnp.float32).astype(jnp.bfloat16)
            parts.append(source[:, pl.ds(start, 128)] * sign)
        return jnp.concatenate(parts, axis=1)

    for copy in copies[:4]:
        copy.wait()
    in_sum = jnp.zeros((rows, 128), jnp.float32)
    step = 4
    for b in range(0, in_tiles.shape[0], step):
        in_sum += jnp.dot(
            gathered(acts, in_blocks, in_signs, b, step),
            in_tiles[b : b + step].reshape(step * 128, 128),
            preferred_element_type=jnp.float32,
        )
    copies[4].wait()
    row = lax.broadcasted_iota(jnp.int32, (rows, 128), 0)
    limit = jnp.full((rows, 128), lengths[0], jnp.int32)
    for e in range(1, examples):
        limit = jnp.where(row >= e * seq_dev, lengths[e], limit)
    live = (row % seq_dev + offset) < limit
    in_sketched = jnp.where(live, in_sum, 0.0).astype(jnp.bfloat16)
    src = lax.broadcasted_iota(jnp.int32, (128, 128), 1)
    dst = lax.broadcasted_iota(jnp.int32, (128, 128), 0)
    pick = (src == (dst // 64) * 64 + 2 * (dst % 32) + (dst // 32) % 2).astype(jnp.bfloat16)
    in_turned = lax.dot_general(pick, in_sketched, NT, preferred_element_type=jnp.float32)
    in_turned = in_turned.astype(jnp.bfloat16)

    for copy in copies[5:]:
        copy.wait()
    out_twice = []
    for first, last in ((0, in_tiles.shape[0]), (in_tiles.shape[0], out_tiles.shape[0])):
        out_sum = jnp.zeros((rows, 128), jnp.float32)
        for b in range(first, last, step):
            tile = jnp.concatenate([out_tiles[b + i] for i in range(step)], axis=1)
            out_sum += lax.dot_general(
                gathered(grads, out_blocks, out_signs, b, step),
                jnp.concatenate([tile, tile], axis=0),
                NT,
                preferred_element_type=jnp.float32,
            )
        out_twice.append(out_sum.astype(jnp.bfloat16))
    lane = lax.broadcasted_iota(jnp.int32, (32, 128), 1)
    for e in range(examples):
        at = slice(e * seq_dev, (e + 1) * seq_dev)
        for layer in range(2):
            both = jnp.dot(
                in_turned[layer * 64 : (layer + 1) * 64, at],
                out_twice[layer][at, :],
                preferred_element_type=jnp.float32,
            )
            flat = jnp.where(lane < 64, both[:32], both[32:])
            for j in range(4):
                partial_ref[layer * 4 + j, e * 8 : (e + 1) * 8, :] = flat[8 * j : 8 * j + 8]


def score_kernel(kept_ref, other_ref, *refs):
    queries, mine_ref, theirs_ref = refs[:-2], refs[-2], refs[-1]
    block = lax.axis_index("ex") % len(queries)
    total = None
    for m, query in enumerate(queries):
        at = lax.bitwise_xor(block, m)
        rows = jnp.concatenate([kept_ref[at], other_ref[at]], axis=0).astype(jnp.float32)
        row = lax.broadcasted_iota(jnp.int32, rows.shape, 0)
        spread = jnp.concatenate(
            [jnp.where(row % 8 == r, rows, 0.0) for r in range(8)], axis=1
        ).astype(jnp.bfloat16)
        part = lax.dot_general(spread, query[...], NT, preferred_element_type=jnp.float32)
        total = part if total is None else total + part
    scores = total.reshape(total.shape[0] // 8, 8, total.shape[1]).sum(1)
    mine_ref[...] = scores[: mine_ref.shape[0]]
    theirs_ref[...] = scores[mine_ref.shape[0] :]


def swap(x, axis, mask):
    size = lax.axis_size(axis)
    return lax.ppermute(x, axis, [(i, i ^ mask) for i in range(size)])


def per_device(
    acts,
    out_grads,
    lengths,
    in_tiles,
    in_blocks,
    in_signs,
    out_tiles,
    out_blocks,
    out_signs,
    query_grads,
):
    examples_dev, seq_dev, width = acts.shape
    rows = examples_dev * seq_dev
    across = swap(query_grads, "ex", 1)
    beside = swap(query_grads, "ex", 2)
    operands = (
        acts.reshape(rows, width),
        out_grads.reshape(rows, -1),
        lengths,
        in_tiles,
        in_blocks,
        in_signs,
        jnp.swapaxes(out_tiles, 1, 2),
        out_blocks,
        out_signs,
    )
    in_smem = (2, 4, 7)
    total = pl.pallas_call(
        sketch_kernel,
        out_shape=jax.ShapeDtypeStruct((8, examples_dev * 8, 128), jnp.float32),
        in_specs=[pl.BlockSpec(memory_space=pltpu.HBM)] * len(operands),
        out_specs=pl.BlockSpec(memory_space=pltpu.VMEM),
        scratch_shapes=[
            (pltpu.SMEM if i in in_smem else pltpu.VMEM)(x.shape, x.dtype)
            for i, x in enumerate(operands)
        ]
        + [pltpu.SemaphoreType.DMA((len(operands),))],
        compiler_params=pltpu.CompilerParams(vmem_limit_bytes=VMEM_LIMIT),
        name="sketch",
    )(*[pltpu.with_memory_space_constraint(x, pltpu.HBM) for x in operands])
    for mask in (1, 8, 24):
        total = total + swap(total, "seq", mask)
    total, across = lax.optimization_barrier((total, across))
    both = swap(across, "ex", 2)
    total = total + swap(total, "seq", 2)
    total, beside = lax.optimization_barrier((total, beside))
    total = total + swap(total, "seq", 4)
    half = lax.axis_index("ex") // 4
    train = total.reshape(8, examples_dev, 8, 128) / lengths.astype(jnp.float32)[None, :, None, None]
    train = train.astype(jnp.bfloat16).reshape(2, 4, examples_dev * 8, 128)
    kept = lax.dynamic_index_in_dim(train, half, 0, keepdims=False)
    sent = lax.dynamic_index_in_dim(train, 1 - half, 0, keepdims=False)
    other = swap(sent, "ex", 6)
    queries = (query_grads, across, beside, both)
    scores = jax.ShapeDtypeStruct((examples_dev, query_grads.shape[0]), jnp.float32)
    mine, theirs = pl.pallas_call(
        score_kernel,
        out_shape=(scores, scores),
        in_specs=[pl.BlockSpec(memory_space=pltpu.VMEM)] * 6,
        out_specs=(pl.BlockSpec(memory_space=pltpu.VMEM),) * 2,
        compiler_params=pltpu.CompilerParams(vmem_limit_bytes=SCORE_VMEM),
        name="score",
    )(kept, other, *queries)
    return mine + swap(theirs, "ex", 6)


def solution(mesh):
    in_specs = (
        P("ex", "seq", None),
        P("ex", "seq", None),
        P("ex"),
        P(),
        P(),
        P(),
        P(),
        P(),
        P(),
        P("seq", "ex"),
    )
    out_specs = P("ex", "seq")
    return jax.shard_map(
        per_device, mesh=mesh, in_specs=in_specs, out_specs=out_specs, check_vma=False
    )
```

```python
import functools

import jax
import jax.numpy as jnp
from jax import lax
from jax.experimental import pallas as pl
from jax.experimental.pallas import tpu as pltpu
from jax.sharding import PartitionSpec as P

VMEM_LIMIT = 16 * 1024 * 1024
SCORE_VMEM = 8 * 1024 * 1024
C1, C2 = 1750000000, 400000000
NT = (((1,), (1,)), ((), ()))


def sketch_kernel(
    acts_hbm,
    grads_hbm,
    lengths_hbm,
    in_tiles_hbm,
    in_blocks_hbm,
    in_signs_hbm,
    out_tiles_hbm,
    out_blocks_hbm,
    out_signs_hbm,
    partial_ref,
    divisor_ref,
    acts,
    grads,
    lengths,
    in_tiles,
    in_blocks,
    in_signs,
    out_tiles,
    out_blocks,
    out_signs,
    sems,
):
    pairs = (
        (in_blocks_hbm, in_blocks),
        (in_signs_hbm, in_signs),
        (acts_hbm, acts),
        (in_tiles_hbm, in_tiles),
        (lengths_hbm, lengths),
        (out_blocks_hbm, out_blocks),
        (out_signs_hbm, out_signs),
        (grads_hbm, grads),
        (out_tiles_hbm, out_tiles),
    )
    copies = [pltpu.make_async_copy(src, dst, sems.at[i]) for i, (src, dst) in enumerate(pairs)]
    for copy in copies:
        copy.start()
    rows = acts.shape[0]
    examples = lengths.shape[0]
    seq_dev = rows // examples
    offset = lax.axis_index("seq") * seq_dev

    def gathered(source, blocks, signs, first, count):
        parts = []
        for b in range(first, first + count):
            start = pl.multiple_of(blocks[b] * 128, 128)
            sign = (2 * signs[b : b + 1, :] - 1).astype(jnp.float32).astype(jnp.bfloat16)
            parts.append(source[:, pl.ds(start, 128)] * sign)
        return jnp.concatenate(parts, axis=1)

    for copy in copies[:4]:
        copy.wait()
    in_sum = jnp.zeros((rows, 128), jnp.float32)
    step = 4
    for b in range(0, in_tiles.shape[0], step):
        in_sum += jnp.dot(
            gathered(acts, in_blocks, in_signs, b, step),
            in_tiles[b : b + step].reshape(step * 128, 128),
            preferred_element_type=jnp.float32,
        )
    copies[4].wait()
    row = lax.broadcasted_iota(jnp.int32, (rows, 128), 0)
    limit = jnp.full((rows, 128), lengths[0], jnp.int32)
    for e in range(1, examples):
        limit = jnp.where(row >= e * seq_dev, lengths[e], limit)
    for e in range(examples):
        divisor_ref[e * 8 : (e + 1) * 8, :] = jnp.full((8, 128), lengths[e], jnp.int32).astype(
            jnp.float32
        )
    live = (row % seq_dev + offset) < limit
    in_sketched = jnp.where(live, in_sum, 0.0).astype(jnp.bfloat16)
    src = lax.broadcasted_iota(jnp.int32, (128, 128), 1)
    dst = lax.broadcasted_iota(jnp.int32, (128, 128), 0)
    pick = (src == (dst // 64) * 64 + 2 * (dst % 32) + (dst // 32) % 2).astype(jnp.bfloat16)
    in_turned = lax.dot_general(pick, in_sketched, NT, preferred_element_type=jnp.float32)
    in_turned = in_turned.astype(jnp.bfloat16)

    for copy in copies[5:]:
        copy.wait()
    out_twice = []
    for first, last in ((0, in_tiles.shape[0]), (in_tiles.shape[0], out_tiles.shape[0])):
        out_sum = jnp.zeros((rows, 128), jnp.float32)
        for b in range(first, last, step):
            tile = jnp.concatenate([out_tiles[b + i] for i in range(step)], axis=1)
            out_sum += lax.dot_general(
                gathered(grads, out_blocks, out_signs, b, step),
                jnp.concatenate([tile, tile], axis=0),
                NT,
                preferred_element_type=jnp.float32,
            )
        out_twice.append(out_sum.astype(jnp.bfloat16))
    lane = lax.broadcasted_iota(jnp.int32, (32, 128), 1)
    for e in range(examples):
        at = slice(e * seq_dev, (e + 1) * seq_dev)
        for layer in range(2):
            both = jnp.dot(
                in_turned[layer * 64 : (layer + 1) * 64, at],
                out_twice[layer][at, :],
                preferred_element_type=jnp.float32,
            )
            flat = jnp.where(lane < 64, both[:32], both[32:])
            for j in range(4):
                partial_ref[layer * 4 + j, e * 8 : (e + 1) * 8, :] = flat[8 * j : 8 * j + 8]


def score_kernel(kept_ref, other_ref, *refs):
    queries, mine_ref, theirs_ref = refs[:-2], refs[-2], refs[-1]
    block = lax.axis_index("ex") % len(queries)
    total = None
    for m, query in enumerate(queries):
        at = lax.bitwise_xor(block, m)
        rows = jnp.concatenate([kept_ref[at], other_ref[at]], axis=0).astype(jnp.float32)
        row = lax.broadcasted_iota(jnp.int32, rows.shape, 0)
        spread = jnp.concatenate(
            [jnp.where(row % 8 == r, rows, 0.0) for r in range(8)], axis=1
        ).astype(jnp.bfloat16)
        part = lax.dot_general(spread, query[...], NT, preferred_element_type=jnp.float32)
        total = part if total is None else total + part
    scores = total.reshape(total.shape[0] // 8, 8, total.shape[1]).sum(1)
    mine_ref[...] = scores[: mine_ref.shape[0]]
    theirs_ref[...] = scores[mine_ref.shape[0] :]


def swap(x, axis, mask):
    size = lax.axis_size(axis)
    return lax.ppermute(x, axis, [(i, i ^ mask) for i in range(size)])


def add_kernel(x_ref, y_ref, sum_ref, sent_ref):
    total = x_ref[...] + y_ref[...].astype(jnp.float32)
    sum_ref[...] = total
    sent_ref[...] = total.astype(jnp.bfloat16)


def added(x, y, cost=0):
    return pl.pallas_call(
        add_kernel,
        out_shape=(
            jax.ShapeDtypeStruct(x.shape, jnp.float32),
            jax.ShapeDtypeStruct(x.shape, jnp.bfloat16),
        ),
        in_specs=[pl.BlockSpec(memory_space=pltpu.VMEM)] * 2,
        out_specs=(pl.BlockSpec(memory_space=pltpu.VMEM),) * 2,
        cost_estimate=pl.CostEstimate(flops=cost, bytes_accessed=cost, transcendentals=0),
        compiler_params=pltpu.CompilerParams(vmem_limit_bytes=SCORE_VMEM),
        name="add",
    )(x, y)


def finish_kernel(x_ref, y_ref, divisor_ref, kept_ref, sent_ref):
    half = lax.axis_index("ex") // 4
    for part, out_ref in ((half, kept_ref), (1 - half, sent_ref)):
        at = pl.ds(part * 4, 4)
        total = x_ref[at] + y_ref[at].astype(jnp.float32)
        out_ref[...] = (total / divisor_ref[...][None]).astype(jnp.bfloat16)


def finished(x, y, divisor, cost):
    half = jax.ShapeDtypeStruct((x.shape[0] // 2,) + x.shape[1:], jnp.bfloat16)
    return pl.pallas_call(
        finish_kernel,
        out_shape=(half, half),
        in_specs=[pl.BlockSpec(memory_space=pltpu.VMEM)] * 3,
        out_specs=(pl.BlockSpec(memory_space=pltpu.VMEM),) * 2,
        cost_estimate=pl.CostEstimate(flops=cost, bytes_accessed=cost, transcendentals=0),
        compiler_params=pltpu.CompilerParams(vmem_limit_bytes=SCORE_VMEM),
        name="finish",
    )(x, y, divisor)


def per_device(
    acts,
    out_grads,
    lengths,
    in_tiles,
    in_blocks,
    in_signs,
    out_tiles,
    out_blocks,
    out_signs,
    query_grads,
):
    examples_dev, seq_dev, width = acts.shape
    rows = examples_dev * seq_dev
    across = swap(query_grads, "ex", 1)
    beside = swap(query_grads, "ex", 2)
    operands = (
        acts.reshape(rows, width),
        out_grads.reshape(rows, -1),
        lengths,
        in_tiles,
        in_blocks,
        in_signs,
        jnp.swapaxes(out_tiles, 1, 2),
        out_blocks,
        out_signs,
    )
    in_smem = (2, 4, 7)
    total, divisor = pl.pallas_call(
        sketch_kernel,
        out_shape=(
            jax.ShapeDtypeStruct((8, examples_dev * 8, 128), jnp.float32),
            jax.ShapeDtypeStruct((examples_dev * 8, 128), jnp.float32),
        ),
        in_specs=[pl.BlockSpec(memory_space=pltpu.HBM)] * len(operands),
        out_specs=(pl.BlockSpec(memory_space=pltpu.VMEM),) * 2,
        scratch_shapes=[
            (pltpu.SMEM if i in in_smem else pltpu.VMEM)(x.shape, x.dtype)
            for i, x in enumerate(operands)
        ]
        + [pltpu.SemaphoreType.DMA((len(operands),))],
        cost_estimate=pl.CostEstimate(flops=10**9, bytes_accessed=10**7, transcendentals=0),
        compiler_params=pltpu.CompilerParams(vmem_limit_bytes=VMEM_LIMIT),
        name="sketch",
    )(*[pltpu.with_memory_space_constraint(x, pltpu.HBM) for x in operands])
    total, sent = added(total, swap(total, "seq", 1))
    total, sent = added(total, swap(sent, "seq", 9))
    total, sent = added(total, swap(sent, "seq", 25))
    both = swap(across, "ex", 2)
    total, sent = added(total, swap(sent, "seq", 3), C1)
    total, sent, beside = lax.optimization_barrier((total, sent, beside))
    kept, sent = finished(total, swap(sent, "seq", 5), divisor, C2)
    seq, ex = lax.axis_size("seq"), lax.axis_size("ex")
    other = lax.ppermute(
        sent,
        ("seq", "ex"),
        [(i * ex + j, (i ^ 1) * ex + (j ^ 6)) for i in range(seq) for j in range(ex)],
    )
    other, both = lax.optimization_barrier((other, both))
    queries = (query_grads, across, beside, both)
    scores = jax.ShapeDtypeStruct((examples_dev, query_grads.shape[0]), jnp.float32)
    mine, theirs = pl.pallas_call(
        score_kernel,
        out_shape=(scores, scores),
        in_specs=[pl.BlockSpec(memory_space=pltpu.VMEM)] * 6,
        out_specs=(pl.BlockSpec(memory_space=pltpu.VMEM),) * 2,
        compiler_params=pltpu.CompilerParams(vmem_limit_bytes=SCORE_VMEM),
        name="score",
    )(kept, other, *queries)
    return mine + swap(theirs, "ex", 6)


def solution(mesh):
    in_specs = (
        P("ex", "seq", None),
        P("ex", "seq", None),
        P("ex"),
        P(),
        P(),
        P(),
        P(),
        P(),
        P(),
        P("seq", "ex"),
    )
    out_specs = P("ex", "seq")
    return jax.shard_map(
        per_device, mesh=mesh, in_specs=in_specs, out_specs=out_specs, check_vma=False
    )
```

```python
import functools

import jax
import jax.numpy as jnp
from jax import lax
from jax.experimental import pallas as pl
from jax.experimental.pallas import tpu as pltpu
from jax.sharding import PartitionSpec as P

VMEM_LIMIT = 16 * 1024 * 1024
SCORE_VMEM = 8 * 1024 * 1024
C1, C2 = 1750000000, 400000000
NT = (((1,), (1,)), ((), ()))


def sketch_kernel(
    acts_hbm,
    grads_hbm,
    lengths_hbm,
    in_tiles_hbm,
    in_blocks_hbm,
    in_signs_hbm,
    out_tiles_hbm,
    out_blocks_hbm,
    out_signs_hbm,
    partial_ref,
    divisor_ref,
    acts,
    grads,
    lengths,
    in_tiles,
    in_blocks,
    in_signs,
    out_tiles,
    out_blocks,
    out_signs,
    sems,
):
    pairs = (
        (in_blocks_hbm, in_blocks),
        (in_signs_hbm, in_signs),
        (acts_hbm, acts),
        (in_tiles_hbm, in_tiles),
        (lengths_hbm, lengths),
        (out_blocks_hbm, out_blocks),
        (out_signs_hbm, out_signs),
        (grads_hbm, grads),
        (out_tiles_hbm, out_tiles),
    )
    copies = [pltpu.make_async_copy(src, dst, sems.at[i]) for i, (src, dst) in enumerate(pairs)]
    for copy in copies:
        copy.start()
    rows = acts.shape[0]
    examples = lengths.shape[0]
    seq_dev = rows // examples
    offset = lax.axis_index("seq") * seq_dev

    def gathered(source, blocks, signs, first, count):
        parts = []
        for b in range(first, first + count):
            start = pl.multiple_of(blocks[b] * 128, 128)
            sign = (2 * signs[b : b + 1, :] - 1).astype(jnp.float32).astype(jnp.bfloat16)
            parts.append(source[:, pl.ds(start, 128)] * sign)
        return jnp.concatenate(parts, axis=1)

    for copy in copies[:4]:
        copy.wait()
    in_sum = jnp.zeros((rows, 128), jnp.float32)
    step = 4
    for b in range(0, in_tiles.shape[0], step):
        in_sum += jnp.dot(
            gathered(acts, in_blocks, in_signs, b, step),
            in_tiles[b : b + step].reshape(step * 128, 128),
            preferred_element_type=jnp.float32,
        )
    copies[4].wait()
    row = lax.broadcasted_iota(jnp.int32, (rows, 128), 0)
    limit = jnp.full((rows, 128), lengths[0], jnp.int32)
    for e in range(1, examples):
        limit = jnp.where(row >= e * seq_dev, lengths[e], limit)
    for e in range(examples):
        divisor_ref[e * 8 : (e + 1) * 8, :] = jnp.full((8, 128), lengths[e], jnp.int32).astype(
            jnp.float32
        )
    live = (row % seq_dev + offset) < limit
    in_sketched = jnp.where(live, in_sum, 0.0).astype(jnp.bfloat16)
    src = lax.broadcasted_iota(jnp.int32, (128, 128), 1)
    dst = lax.broadcasted_iota(jnp.int32, (128, 128), 0)
    pick = (src == (dst // 64) * 64 + 2 * (dst % 32) + (dst // 32) % 2).astype(jnp.bfloat16)
    in_turned = lax.dot_general(pick, in_sketched, NT, preferred_element_type=jnp.float32)
    in_turned = in_turned.astype(jnp.bfloat16)

    for copy in copies[5:]:
        copy.wait()
    out_twice = []
    for first, last in ((0, in_tiles.shape[0]), (in_tiles.shape[0], out_tiles.shape[0])):
        out_sum = jnp.zeros((rows, 128), jnp.float32)
        for b in range(first, last, step):
            tile = jnp.concatenate([out_tiles[b + i] for i in range(step)], axis=1)
            out_sum += lax.dot_general(
                gathered(grads, out_blocks, out_signs, b, step),
                jnp.concatenate([tile, tile], axis=0),
                NT,
                preferred_element_type=jnp.float32,
            )
        out_twice.append(out_sum.astype(jnp.bfloat16))
    lane = lax.broadcasted_iota(jnp.int32, (32, 128), 1)
    for e in range(examples):
        at = slice(e * seq_dev, (e + 1) * seq_dev)
        for layer in range(2):
            both = jnp.dot(
                in_turned[layer * 64 : (layer + 1) * 64, at],
                out_twice[layer][at, :],
                preferred_element_type=jnp.float32,
            )
            flat = jnp.where(lane < 64, both[:32], both[32:])
            for j in range(4):
                partial_ref[layer * 4 + j, e * 8 : (e + 1) * 8, :] = flat[8 * j : 8 * j + 8]


def score_kernel(kept_ref, other_ref, *refs):
    queries, mine_ref, theirs_ref = refs[:-2], refs[-2], refs[-1]
    ex = lax.axis_index("ex")
    block = ex % 2 + 2 * (ex // 4)
    total = None
    for m, query in enumerate(queries):
        at = lax.bitwise_xor(block, m)
        rows = jnp.concatenate([kept_ref[at], other_ref[at]], axis=0).astype(jnp.float32)
        row = lax.broadcasted_iota(jnp.int32, rows.shape, 0)
        spread = jnp.concatenate(
            [jnp.where(row % 8 == r, rows, 0.0) for r in range(8)], axis=1
        ).astype(jnp.bfloat16)
        part = lax.dot_general(spread, query[...], NT, preferred_element_type=jnp.float32)
        total = part if total is None else total + part
    scores = total.reshape(total.shape[0] // 8, 8, total.shape[1]).sum(1)
    mine_ref[...] = scores[: mine_ref.shape[0]]
    theirs_ref[...] = scores[mine_ref.shape[0] :]


def swap(x, axis, mask):
    size = lax.axis_size(axis)
    return lax.ppermute(x, axis, [(i, i ^ mask) for i in range(size)])


def add_kernel(x_ref, y_ref, sum_ref, sent_ref):
    total = x_ref[...] + y_ref[...].astype(jnp.float32)
    sum_ref[...] = total
    sent_ref[...] = total.astype(jnp.bfloat16)


def added(x, y, cost=0):
    return pl.pallas_call(
        add_kernel,
        out_shape=(
            jax.ShapeDtypeStruct(x.shape, jnp.float32),
            jax.ShapeDtypeStruct(x.shape, jnp.bfloat16),
        ),
        in_specs=[pl.BlockSpec(memory_space=pltpu.VMEM)] * 2,
        out_specs=(pl.BlockSpec(memory_space=pltpu.VMEM),) * 2,
        cost_estimate=pl.CostEstimate(flops=cost, bytes_accessed=cost, transcendentals=0),
        compiler_params=pltpu.CompilerParams(vmem_limit_bytes=SCORE_VMEM),
        name="add",
    )(x, y)


def finish_kernel(x_ref, y_ref, divisor_ref, kept_ref, sent_ref):
    ex = lax.axis_index("ex")
    inner = (ex // 2 + ex // 4) % 2
    for part, out_ref in ((inner, kept_ref), (1 - inner, sent_ref)):
        for i, first in enumerate((2 * part, 6 - 2 * part)):
            at = pl.ds(first, 2)
            total = x_ref[at] + y_ref[at].astype(jnp.float32)
            out_ref[2 * i : 2 * i + 2] = (total / divisor_ref[...][None]).astype(jnp.bfloat16)


def finished(x, y, divisor, cost):
    half = jax.ShapeDtypeStruct((x.shape[0] // 2,) + x.shape[1:], jnp.bfloat16)
    return pl.pallas_call(
        finish_kernel,
        out_shape=(half, half),
        in_specs=[pl.BlockSpec(memory_space=pltpu.VMEM)] * 3,
        out_specs=(pl.BlockSpec(memory_space=pltpu.VMEM),) * 2,
        cost_estimate=pl.CostEstimate(flops=cost, bytes_accessed=cost, transcendentals=0),
        compiler_params=pltpu.CompilerParams(vmem_limit_bytes=SCORE_VMEM),
        name="finish",
    )(x, y, divisor)


def per_device(
    acts,
    out_grads,
    lengths,
    in_tiles,
    in_blocks,
    in_signs,
    out_tiles,
    out_blocks,
    out_signs,
    query_grads,
):
    examples_dev, seq_dev, width = acts.shape
    rows = examples_dev * seq_dev
    across = swap(query_grads, "ex", 1)
    beside = swap(query_grads, "ex", 6)
    operands = (
        acts.reshape(rows, width),
        out_grads.reshape(rows, -1),
        lengths,
        in_tiles,
        in_blocks,
        in_signs,
        jnp.swapaxes(out_tiles, 1, 2),
        out_blocks,
        out_signs,
    )
    in_smem = (2, 4, 7)
    total, divisor = pl.pallas_call(
        sketch_kernel,
        out_shape=(
            jax.ShapeDtypeStruct((8, examples_dev * 8, 128), jnp.float32),
            jax.ShapeDtypeStruct((examples_dev * 8, 128), jnp.float32),
        ),
        in_specs=[pl.BlockSpec(memory_space=pltpu.HBM)] * len(operands),
        out_specs=(pl.BlockSpec(memory_space=pltpu.VMEM),) * 2,
        scratch_shapes=[
            (pltpu.SMEM if i in in_smem else pltpu.VMEM)(x.shape, x.dtype)
            for i, x in enumerate(operands)
        ]
        + [pltpu.SemaphoreType.DMA((len(operands),))],
        cost_estimate=pl.CostEstimate(flops=10**9, bytes_accessed=10**7, transcendentals=0),
        compiler_params=pltpu.CompilerParams(vmem_limit_bytes=VMEM_LIMIT),
        name="sketch",
    )(*[pltpu.with_memory_space_constraint(x, pltpu.HBM) for x in operands])
    total, sent = added(total, swap(total, "seq", 1))
    total, sent = added(total, swap(sent, "seq", 9))
    total, sent = added(total, swap(sent, "seq", 25))
    both = swap(across, "ex", 6)
    total, sent = added(total, swap(sent, "seq", 5), C1)
    total, sent, beside = lax.optimization_barrier((total, sent, beside))
    kept, sent = finished(total, swap(sent, "seq", 3), divisor, C2)
    seq, ex = lax.axis_size("seq"), lax.axis_size("ex")
    other = lax.ppermute(
        sent,
        ("seq", "ex"),
        [(i * ex + j, (i ^ 1) * ex + (j ^ 2)) for i in range(seq) for j in range(ex)],
    )
    other, both = lax.optimization_barrier((other, both))
    queries = (query_grads, across, beside, both)
    scores = jax.ShapeDtypeStruct((examples_dev, query_grads.shape[0]), jnp.float32)
    mine, theirs = pl.pallas_call(
        score_kernel,
        out_shape=(scores, scores),
        in_specs=[pl.BlockSpec(memory_space=pltpu.VMEM)] * 6,
        out_specs=(pl.BlockSpec(memory_space=pltpu.VMEM),) * 2,
        compiler_params=pltpu.CompilerParams(vmem_limit_bytes=SCORE_VMEM),
        name="score",
    )(kept, other, *queries)
    return mine + swap(theirs, "ex", 2)


def solution(mesh):
    in_specs = (
        P("ex", "seq", None),
        P("ex", "seq", None),
        P("ex"),
        P(),
        P(),
        P(),
        P(),
        P(),
        P(),
        P("seq", "ex"),
    )
    out_specs = P("ex", "seq")
    return jax.shard_map(
        per_device, mesh=mesh, in_specs=in_specs, out_specs=out_specs, check_vma=False
    )
```
